128 devices in a mesh: dp: 8 (over z, core), vocab: 16 (over y, x).
Axes of the slice: x: 4, y: 4, z: 4, core: 2. Of those that a mesh axis runs over, the one named last changes fastest.
Arguments:
- hidden: bfloat16 [2048, 8192], P('dp', 'vocab'), may hold values from -3 to 3
- head: bfloat16 [65536, 8192], P(('vocab', 'dp')), may hold values from -0.9 to 0.9
- block_lists: int32 [16, 16], replicated, may hold values from 0 to 127, as said below
- target_slot: int32 [2048], replicated, may hold values from 0 to 8191
- loss_grad: float32 [2048], P('dp'), may hold values from 2 to 6
Outputs:
- losses: float32 [2048], P('dp')
- hidden_grad: bfloat16 [2048, 8192], P('dp', 'vocab')
- head_grad: bfloat16 [65536, 8192], P(('vocab', 'dp'))
The draws below stay inside these ranges and needn't reach their ends.
Inputs may be any that keep to these rules, and one draw needn't show every extreme that they name: `block_lists`: within one row the 16 blocks are distinct; among the 2 token blocks of one dp index no vocabulary block is listed twice; one vocabulary block is listed by a token block of every dp index.
All inputs are finite; a program needn't handle non-finite values.
Results may differ from the reference program's by a relative error of at most 0.014.
Values may be sent and summed in bfloat16 or wider, within the bound.
No kernel may reach another device: no remote copies, remote signals or barrier semaphores. Data moves between devices by JAX's collectives and lax.ppermute only.
A program may use at most 576 MiB of HBM per device.

```python
import jax
import jax.numpy as jnp
from jax import lax

D = 8192
BV = 512
BLK = 128
VB = 128
VOCAB = 65536
K = 16
TB_ROW = 2
TBLOCKS = 16
TOKENS = 2048


def pick_lists(key):
    key = jax.random.fold_in(key, 7)
    order = jax.random.permutation(jax.random.fold_in(key, 1), VB).astype(jnp.int32)
    bias = (VB - 1 - order) * (VB - 1 - order) * 8192 // (VB * VB)
    bias = bias + jnp.where(order == 0, 1048576, 0)
    noise = jax.random.randint(jax.random.fold_in(key, 2), (TBLOCKS // TB_ROW, VB), 0, 4096)
    score = (noise + bias[None, :]) * VB + jnp.arange(VB, dtype=jnp.int32)[None, :]
    unused, picked = lax.top_k(score, TB_ROW * K)
    return picked.reshape(TBLOCKS, K).astype(jnp.int32)


def head_values(key):
    values = jax.random.normal(jax.random.fold_in(key, 5), (VOCAB, D), jnp.float32)
    return 0.18 * jnp.clip(values, -5.0, 5.0)


def draw_block_lists(key, part):
    return pick_lists(key)


def draw_head(key, part):
    return head_values(key).astype(jnp.bfloat16)


def draw_hidden(key, part):
    key = jax.random.fold_in(key, 3)
    base = 0.18 * jnp.clip(jax.random.normal(jax.random.fold_in(key, 1), (TOKENS, D), jnp.float32), -5.0, 5.0)
    return base.astype(jnp.bfloat16)


def with_ends(entries, key, least, largest):
    longest = entries.shape.index(max(entries.shape))
    spots = []
    for shift in (0, 1):
        where = [jax.random.randint(jax.random.fold_in(key, axis), (), 0, length) for axis, length in enumerate(entries.shape)]
        where[longest] = (where[longest] + shift) % entries.shape[longest]
        spots.append(tuple(where))
    return entries.at[spots[0]].set(least).at[spots[1]].set(largest)


def steps_of(rng, shape, shards, smallest, high):
    gain = 1.0
    for dim, blocks in shards:
        steps = jax.random.uniform(jax.random.fold_in(jax.random.fold_in(rng, 6), dim), (blocks,), jnp.float32, smallest / len(shards), high / len(shards))
        gain = gain * jnp.repeat(jnp.exp(steps), shape[dim] // blocks).reshape((-1,) + (1,) * (len(shape) - 1 - dim))
    return gain


def setup_inputs(seed: int = 0) -> dict:
    keys = jax.random.split(jax.random.key(seed), 6)
    hidden = draw_hidden(jax.random.fold_in(keys[5], 71), 0)
    head = draw_head(jax.random.fold_in(keys[5], 71), 0)
    block_lists = draw_block_lists(jax.random.fold_in(keys[5], 71), 0)
    target_slot = with_ends(jax.random.randint(keys[3], (TOKENS,), 0, K * BV), jax.random.fold_in(keys[3], 1), 0, (K * BV) - 1).astype(jnp.int32)
    loss_grad = jnp.clip(2.0 + 4.0 * jax.random.uniform(keys[4], (TOKENS,), jnp.float32) ** steps_of(keys[4], (TOKENS,), ((0, 8),), -0.2, 0.2), 2.0, 6.0)
    return {"hidden": hidden, "head": head, "block_lists": block_lists, "target_slot": target_slot, "loss_grad": loss_grad}


def reference(hidden, head, block_lists, target_slot, loss_grad):
    groups = TBLOCKS // TB_ROW
    h_blocks = hidden.reshape(TBLOCKS, BLK, D)
    head_blocks = head.reshape(VB, BV, D)
    slot_blocks = target_slot.reshape(TBLOCKS, BLK)
    grad_blocks = loss_grad.reshape(TBLOCKS, BLK)
    columns = jnp.arange(K * BV, dtype=jnp.int32)

    def one_block(pack):
        rows, names, slots, weights = pack
        chosen = jnp.take(head_blocks, names, axis=0).reshape(K * BV, D)
        logits = jnp.dot(rows, chosen.T, preferred_element_type=jnp.float32)
        top = jnp.max(logits, axis=1)
        lse = top + jnp.log(jnp.sum(jnp.exp(logits - top[:, None]), axis=1))
        picked = jnp.take_along_axis(logits, slots[:, None], axis=1)[:, 0]
        onehot = (columns[None, :] == slots[:, None]).astype(jnp.float32)
        dlogits = (weights[:, None] * (jnp.exp(logits - lse[:, None]) - onehot)).astype(jnp.bfloat16)
        terms = jnp.einsum("tkv,kvd->ktd", dlogits.reshape(BLK, K, BV).astype(jnp.float32),
                           chosen.reshape(K, BV, D).astype(jnp.float32)).astype(jnp.bfloat16)
        summed = jnp.sum(terms.astype(jnp.float32), axis=0).astype(jnp.bfloat16)
        return lse - picked, lse, summed

    losses, lse_all, hidden_grad = lax.map(one_block, (h_blocks, block_lists, slot_blocks, grad_blocks))
    lse_all = lse_all.reshape(TBLOCKS, BLK)
    grouped = block_lists.reshape(groups, TB_ROW, K)
    local_cols = jnp.arange(BV, dtype=jnp.int32)

    def one_vocab(block):
        named = jnp.any(grouped == block, axis=2)
        present = jnp.any(named, axis=1)
        which = jnp.sum(named.astype(jnp.int32) * jnp.arange(TB_ROW, dtype=jnp.int32)[None, :], axis=1)
        index = (jnp.arange(groups, dtype=jnp.int32) * TB_ROW + which).astype(jnp.int32)
        rows = jnp.take(h_blocks, index, axis=0).reshape(groups * BLK, D)
        slots = jnp.take(slot_blocks, index, axis=0)
        lse = jnp.take(lse_all, index, axis=0)
        weights = jnp.take(grad_blocks, index, axis=0) * present[:, None].astype(jnp.float32)
        target_block = jnp.take_along_axis(jnp.take(block_lists, index, axis=0), slots // BV, axis=1)
        target_col = jnp.where(target_block == block, slots % BV, -1)
        weight_rows = lax.dynamic_index_in_dim(head_blocks, block, 0, keepdims=False)
        logits = jnp.dot(rows, weight_rows.T, preferred_element_type=jnp.float32).reshape(groups, BLK, BV)
        onehot = (local_cols[None, None, :] == target_col[:, :, None]).astype(jnp.float32)
        dlogits = (weights[:, :, None] * (jnp.exp(logits - lse[:, :, None]) - onehot)).astype(jnp.bfloat16)
        return jnp.dot(dlogits.reshape(groups * BLK, BV).T, rows, preferred_element_type=jnp.float32).astype(jnp.bfloat16)

    head_grad = lax.map(one_vocab, jnp.arange(VB, dtype=jnp.int32)).reshape(VOCAB, D)
    return losses.reshape(TOKENS), hidden_grad.reshape(TOKENS, D), head_grad
```

```python
import jax
import jax.numpy as jnp
from jax import lax
from jax.experimental import pallas as pl
from jax.experimental.pallas import tpu as pltpu
from jax.sharding import Mesh
from jax.sharding import PartitionSpec as P

BLK = 128
SIDE = 4
CORES = 2
AXES = ("z", "c", "y", "x")
LOW = -1e30
F32 = jnp.float32
BF16 = jnp.bfloat16
bar = lax.optimization_barrier


def signed_pairs(axis, steps):
    pairs = []
    for z in range(SIDE):
        for c in range(CORES):
            for y in range(SIDE):
                for x in range(SIDE):
                    at = {"z": z, "y": y, "x": x}
                    to = dict(at)
                    to[axis] = (at[axis] + (1 - 2 * c) * steps) % SIDE

                    def line(p):
                        return ((p["z"] * CORES + c) * SIDE + p["y"]) * SIDE + p["x"]

                    pairs.append((line(at), line(to)))
    return pairs


def shift(array, axis, steps):
    return lax.ppermute(array, AXES, signed_pairs(axis, steps))


def pick_rows(array, at):
    return jnp.stack(
        [lax.dynamic_index_in_dim(array, at[q], 0, keepdims=False) for q in range(SIDE)]
    )


def swap_cores(array):
    return lax.ppermute(array, "c", [(0, 1), (1, 0)])


def gather_direct(arrays, axes, dims):
    moved = [[shift(a, axis, q) for q in range(1, SIDE)] for a, axis in zip(arrays, axes)]
    moved = bar(moved)
    return [jnp.concatenate([a] + m, dim) for a, m, dim in zip(arrays, moved, dims)]


def scatter_direct(arrays, axes, dims):
    parts = [jnp.split(a, SIDE, dim) for a, dim in zip(arrays, dims)]
    moved = [
        [shift(p[q], axis, -q) for q in range(1, SIDE)] for p, axis in zip(parts, axes)
    ]
    moved = bar(moved)
    return [
        (p[0].astype(F32) + m[0].astype(F32) + m[1].astype(F32) + m[2].astype(F32)).astype(BF16)
        for p, m in zip(parts, moved)
    ]


def params():
    return pltpu.CompilerParams(vmem_limit_bytes=40 * 2**20)


def cost(flops, bytes_accessed):
    return pl.CostEstimate(flops=flops, bytes_accessed=bytes_accessed, transcendentals=0)


NT = (((1,), (1,)), ((), ()))


def logits_part(x, own, sib, index, before=None):
    rows, depth = x.shape
    vocab, width = own.shape
    f = width // (SIDE * SIDE)
    blocks = depth // f

    def kernel(index_ref, *refs):
        out_ref = refs[-1]
        x_ref, own_ref, sib_ref = refs[:3]
        k = pl.program_id(0)

        @pl.when(k == 0)
        def _():
            out_ref[...] = jnp.zeros_like(out_ref) if before is None else refs[3][...]

        out_ref[:, :vocab] += lax.dot_general(
            x_ref[...], own_ref[...], NT, preferred_element_type=F32
        )
        out_ref[:, vocab:] += lax.dot_general(
            x_ref[...], sib_ref[...], NT, preferred_element_type=F32
        )

    in_specs = [
        pl.BlockSpec((rows, f), lambda k, index_ref: (0, k)),
        pl.BlockSpec((vocab, f), lambda k, index_ref: (0, index_ref[k])),
        pl.BlockSpec((vocab, f), lambda k, index_ref: (0, index_ref[k])),
    ]
    args = [x, own, sib]
    if before is not None:
        in_specs.append(pl.BlockSpec((rows, 2 * vocab), lambda k, index_ref: (0, 0)))
        args.append(before)
    return pl.pallas_call(
        kernel,
        out_shape=jax.ShapeDtypeStruct((rows, 2 * vocab), F32),
        grid_spec=pltpu.PrefetchScalarGridSpec(
            num_scalar_prefetch=1,
            grid=(blocks,),
            in_specs=in_specs,
            out_specs=pl.BlockSpec((rows, 2 * vocab), lambda k, index_ref: (0, 0)),
        ),
        compiler_params=params(),
        cost_estimate=cost(4 * rows * depth * vocab, 4 * vocab * depth + 2 * rows * depth),
    )(index, *args)


def terms_part(dl, own, sib, index):
    rows = dl.shape[0]
    vocab, width = own.shape
    f = width // (SIDE * SIDE)
    blocks = index.shape[0]

    def kernel(index_ref, dl_ref, own_ref, sib_ref, out_ref):
        total = jnp.dot(dl_ref[:, :vocab], own_ref[...], preferred_element_type=F32)
        total += jnp.dot(dl_ref[:, vocab:], sib_ref[...], preferred_element_type=F32)
        out_ref[...] = total.astype(BF16)

    return pl.pallas_call(
        kernel,
        out_shape=jax.ShapeDtypeStruct((rows, blocks * f), BF16),
        grid_spec=pltpu.PrefetchScalarGridSpec(
            num_scalar_prefetch=1,
            grid=(blocks,),
            in_specs=[
                pl.BlockSpec((rows, 2 * vocab), lambda k, index_ref: (0, 0)),
                pl.BlockSpec((vocab, f), lambda k, index_ref: (0, index_ref[k])),
                pl.BlockSpec((vocab, f), lambda k, index_ref: (0, index_ref[k])),
            ],
            out_specs=pl.BlockSpec((rows, f), lambda k, index_ref: (0, k)),
        ),
        compiler_params=params(),
        cost_estimate=cost(
            4 * rows * blocks * f * vocab, 4 * vocab * blocks * f + 2 * rows * blocks * f
        ),
    )(index, dl, own, sib)


def head_part(dls, xa, xb, xc, index, before=None):
    vocab = dls[0].shape[0]
    width = xa.shape[1]
    f = width // (SIDE * SIDE)
    rows = [d.shape[1] for d in dls]

    def kernel(index_ref, *refs):
        da, db, dc, a_ref, b_ref, c_ref = refs[:6]
        out_ref = refs[-1]
        total = jnp.dot(da[...], a_ref[...], preferred_element_type=F32)
        total += jnp.dot(db[...], b_ref[0], preferred_element_type=F32)
        total += jnp.dot(dc[...], c_ref[0], preferred_element_type=F32)
        if before is not None:
            total += refs[6][...].astype(F32)
        out_ref[...] = total.astype(BF16)

    in_specs = [pl.BlockSpec((vocab, r), lambda k, index_ref: (0, 0)) for r in rows]
    in_specs += [
        pl.BlockSpec((rows[0], f), lambda k, index_ref: (0, k)),
        pl.BlockSpec((1, rows[1], f), lambda k, index_ref: (k % SIDE, 0, k // SIDE)),
        pl.BlockSpec((1, rows[2], f), lambda k, index_ref: (k // SIDE, 0, k % SIDE)),
    ]
    args = list(dls) + [xa, xb, xc]
    if before is not None:
        in_specs.append(pl.BlockSpec((vocab, f), lambda k, index_ref: (0, index_ref[k])))
        args.append(before)
    return pl.pallas_call(
        kernel,
        out_shape=jax.ShapeDtypeStruct((vocab, width), BF16),
        grid_spec=pltpu.PrefetchScalarGridSpec(
            num_scalar_prefetch=1,
            grid=(SIDE * SIDE,),
            in_specs=in_specs,
            out_specs=pl.BlockSpec((vocab, f), lambda k, index_ref: (0, index_ref[k])),
        ),
        compiler_params=params(),
        cost_estimate=cost(2 * sum(rows) * vocab * width, 2 * (sum(rows) + vocab) * width),
    )(index, *args)


def on_device(hidden, head, block_lists, target_slot, loss_grad):
    z, c, y, x = (lax.axis_index(a) for a in AXES)
    sign = 1 - 2 * c
    tok, f = hidden.shape
    vocab, width = head.shape
    tb_row = tok // BLK
    groups = SIDE * CORES
    first = 11 * tok // 256 * 8
    second = first
    cuts = (0, first, first + second, tok)
    quarter = jnp.arange(SIDE, dtype=jnp.int32)
    at_z = (z - sign * quarter) % SIDE
    at_y = (y - sign * quarter) % SIDE
    at_x = (x - sign * quarter) % SIDE
    columns = at_y[:, None] * SIDE + at_x[None, :]

    sib = swap_cores(head)

    def by_part(rows_of_dp):
        return jnp.concatenate(
            [rows_of_dp[:, a:b].reshape(-1) for a, b in zip(cuts[:-1], cuts[1:])]
        )

    def by_dp(flat):
        pieces, at = [], 0
        for a, b in zip(cuts[:-1], cuts[1:]):
            pieces.append(flat[at : at + SIDE * (b - a)].reshape(SIDE, b - a))
            at += SIDE * (b - a)
        return jnp.concatenate(pieces, 1)

    dp_at = at_z * CORES + c
    lists = pick_rows(block_lists.reshape(groups, tb_row, -1), dp_at)
    slots = pick_rows(target_slot.reshape(groups, tb_row, BLK), dp_at)
    wanted = jnp.sum(
        jnp.where(
            (slots // vocab)[..., None] == jnp.arange(lists.shape[2], dtype=jnp.int32),
            lists[:, :, None, :],
            0,
        ),
        axis=3,
    )
    base = (y * SIDE + x) * groups + z * CORES
    listed, target = [], []
    for block in (base + c, base + 1 - c):
        named = jnp.any(lists == block, axis=2)
        listed.append(
            by_part(jnp.broadcast_to(named[:, :, None], slots.shape).reshape(SIDE, tok))
        )
        target.append(
            by_part(jnp.where(wanted == block, slots % vocab, -1).reshape(SIDE, tok))
        )

    parts = [hidden[a:b] for a, b in zip(cuts[:-1], cuts[1:])]
    parts = gather_direct(parts, "xyz", (1, 1, 0))
    parts = gather_direct(parts, "yzx", (1, 0, 1))
    chunks = [[p] for p in parts]
    for step in range(SIDE - 1):
        moved = bar([shift(p[-1], axis, 1) for p, axis in zip(chunks, "zxy")])
        for p, m in zip(chunks, moved):
            p.append(m)
    xa, xb, xc = chunks
    every = columns.reshape(-1)
    logits_b = logits_c = None
    for q in range(SIDE):
        logits_b = logits_part(xb[q], head, sib, columns[:, q], logits_b)
        logits_c = logits_part(xc[q], head, sib, columns[q, :], logits_c)
    early = logits_part(jnp.concatenate(xa[:-1], 0), head, sib, every)
    late = logits_part(xa[-1], head, sib, every)
    logits = jnp.concatenate([early, late, logits_b, logits_c], 0)

    local = jnp.arange(vocab, dtype=jnp.int32)
    member = jnp.concatenate(
        [jnp.broadcast_to(l[:, None], (l.shape[0], vocab)) for l in listed], 1
    )
    is_target = jnp.concatenate([t[:, None] == local[None, :] for t in target], 1)
    top = jnp.max(jnp.where(member, logits, LOW), axis=1)
    total = jnp.sum(jnp.where(member, jnp.exp(logits - top[:, None]), 0.0), axis=1)
    pick = jnp.sum(jnp.where(is_target, logits, 0.0), axis=1)

    to_q = (sign * (z - quarter)) % SIDE
    stats = jnp.stack([pick_rows(by_dp(a), to_q) for a in (top, total, pick)])
    flat = jnp.concatenate([stats.reshape(-1), loss_grad])
    count = SIDE**3
    everyone = lax.all_to_all(
        jnp.broadcast_to(flat[None], (count, flat.shape[0])), ("z", "y", "x"), 0, 0, tiled=True
    )
    got = everyone[:, : stats.size].reshape((count,) + stats.shape)
    top_all = jnp.max(got[:, 0], axis=0)
    total_all = jnp.sum(got[:, 1] * jnp.exp(got[:, 0] - top_all), axis=0)
    pick_all = jnp.sum(got[:, 2], axis=0)
    lse_dp = top_all + jnp.log(total_all)
    losses = lax.dynamic_index_in_dim(lse_dp - pick_all, z, 0, keepdims=False)
    weights_dp = everyone[:, stats.size :].reshape(SIDE, SIDE * SIDE, tok)[:, 0]
    lse = by_part(pick_rows(lse_dp, at_z))
    weights = by_part(pick_rows(weights_dp, at_z))

    dl = jnp.where(
        member,
        weights[:, None] * (jnp.exp(logits - lse[:, None]) - is_target.astype(F32)),
        0.0,
    ).astype(BF16)
    ends = [SIDE * e for e in cuts]
    dls = [dl[a:b] for a, b in zip(ends[:-1], ends[1:])]

    ta = terms_part(dls[0], head, sib, every)
    ta = jnp.split(ta, SIDE, 0)

    def own_terms(q):
        return (
            ta[q],
            terms_part(dls[1], head, sib, columns[:, q]),
            terms_part(dls[2], head, sib, columns[q, :]),
        )

    sums = own_terms(1)
    for q in (2, 3, 0):
        moved = bar([shift(s, axis, 1) for s, axis in zip(sums, "zxy")])
        sums = [
            (m.astype(F32) + t.astype(F32)).astype(BF16) for m, t in zip(moved, own_terms(q))
        ]
    sums = scatter_direct(sums, "yzx", (1, 0, 1))
    sums = scatter_direct(sums, "xyz", (1, 1, 0))
    hidden_grad = jnp.concatenate(sums, 0)

    dlt = [d.T for d in dls]
    xa_all, xb_all, xc_all = jnp.concatenate(xa, 0), jnp.stack(xb), jnp.stack(xc)
    theirs = head_part([d[vocab:] for d in dlt], xa_all, xb_all, xc_all, every)
    head_grad = head_part(
        [d[:vocab] for d in dlt], xa_all, xb_all, xc_all, every, swap_cores(theirs)
    )
    return losses, hidden_grad, head_grad


def solution(mesh):
    grid = Mesh(mesh.devices.reshape(SIDE, CORES, SIDE, SIDE), AXES)
    dp, owners = ("z", "c"), ("y", "x")
    in_specs = (P(dp, owners), P(owners + dp, None), P(), P(), P(dp))
    out_specs = (P(dp), P(dp, owners), P(owners + dp, None))
    return jax.shard_map(
        on_device, mesh=grid, in_specs=in_specs, out_specs=out_specs, check_vma=False
    )
```

```python
import jax
import jax.numpy as jnp
from jax import lax
from jax.experimental import pallas as pl
from jax.experimental.pallas import tpu as pltpu
from jax.sharding import Mesh
from jax.sharding import PartitionSpec as P

BLK = 128
SIDE = 4
CORES = 2
AXES = ("z", "c", "y", "x")
LOW = -1e30
VMEM_LIMIT = 48 * 2**20
F32 = jnp.float32
BF16 = jnp.bfloat16
bar = lax.optimization_barrier


def signed_pairs(axis, steps):
    pairs = []
    for z in range(SIDE):
        for c in range(CORES):
            for y in range(SIDE):
                for x in range(SIDE):
                    at = {"z": z, "y": y, "x": x}
                    to = dict(at)
                    to[axis] = (at[axis] + (1 - 2 * c) * steps) % SIDE

                    def line(p):
                        return ((p["z"] * CORES + c) * SIDE + p["y"]) * SIDE + p["x"]

                    pairs.append((line(at), line(to)))
    return pairs


def shift(array, axis, steps):
    return lax.ppermute(array, AXES, signed_pairs(axis, steps))


def pick_rows(array, at):
    return jnp.stack(
        [lax.dynamic_index_in_dim(array, at[q], 0, keepdims=False) for q in range(SIDE)]
    )


def swap_cores(array):
    return lax.ppermute(array, "c", [(0, 1), (1, 0)])


def ring_tick(chunks, axes, beside=()):
    moved = [shift(p[-1], axis, 1) for p, axis in zip(chunks, axes)]
    moved, beside = bar((moved, beside))
    for p, m in zip(chunks, moved):
        p.append(m)
    return beside


def gather_ring(arrays, axes, dims):
    chunks = [[a] for a in arrays]
    for step in range(SIDE - 1):
        ring_tick(chunks, axes)
    return list(bar([jnp.concatenate(p, dim) for p, dim in zip(chunks, dims)]))


def scatter_direct(arrays, axes, dims, beside=()):
    parts = [jnp.split(a, SIDE, dim) for a, dim in zip(arrays, dims)]
    moved = [
        [shift(p[q], axis, -q) for q in range(1, SIDE)] for p, axis in zip(parts, axes)
    ]
    moved, beside = bar((moved, beside))
    sums = [
        (p[0].astype(F32) + m[0].astype(F32) + m[1].astype(F32) + m[2].astype(F32)).astype(BF16)
        for p, m in zip(parts, moved)
    ]
    return sums, beside


def params():
    return pltpu.CompilerParams(vmem_limit_bytes=VMEM_LIMIT)


def cost(flops, bytes_accessed):
    return pl.CostEstimate(flops=flops, bytes_accessed=bytes_accessed, transcendentals=0)


NT = (((1,), (1,)), ((), ()))


def whole(shape):
    return pl.BlockSpec(shape, lambda k, order: (0,) * len(shape))


def slab(shape):
    return pl.BlockSpec(shape, lambda k, order: (0, order[k]))


def column(shape):
    return pl.BlockSpec(shape, lambda k, order: (0, k))


def along_x(order, q, f):
    return pl.ds(pl.multiple_of(order[SIDE + q] * f, f), f)


def statistics(logits, meta):
    vocab = logits.shape[1] // 2
    local = lax.broadcasted_iota(jnp.int32, (logits.shape[0], vocab), 1)
    halves = (logits[:, :vocab], logits[:, vocab:])
    has = [meta[:, h : h + 1] > 0 for h in range(2)]
    tops = [
        jnp.where(n, jnp.max(l, axis=1, keepdims=True), LOW) for n, l in zip(has, halves)
    ]
    top = jnp.maximum(tops[0], tops[1])
    total = pick = 0.0
    for h in range(2):
        total += jnp.where(
            has[h], jnp.sum(jnp.exp(halves[h] - top), axis=1, keepdims=True), 0.0
        )
        pick += jnp.sum(
            jnp.where(local == meta[:, 2 + h : 3 + h], halves[h], 0.0), axis=1, keepdims=True
        )
    found = total > 0
    lse = jnp.where(found, top + jnp.log(jnp.where(found, total, 1.0)), LOW)
    return lse, pick


def logits_tick(q, chunks, own, sib, order, before, metas=None, earlier=()):
    xa, xb, xc = chunks
    ra, rb, rc = (v.shape[0] for v in chunks)
    vocab, width = own.shape
    f = width // (SIDE * SIDE)
    side = f * SIDE
    last = metas is not None
    tok = ra + (rb + rc) // SIDE

    def kernel(order_ref, *refs):
        refs = list(refs)
        a_ref, b_ref, c_ref, own_ref, sib_ref = (refs.pop(0) for _ in range(5))
        before_refs = [refs.pop(0) for _ in before]
        meta_refs = [refs.pop(0) for _ in (metas or ())]
        earlier_refs = [refs.pop(0) for _ in earlier]
        la_ref, lb_ref, lc_ref = (refs.pop(0) for _ in range(3))
        k = pl.program_id(0)

        @pl.when(k == 0)
        def _():
            la_ref[...] = jnp.zeros_like(la_ref)
            lb_ref[...] = before_refs[0][...] if before else jnp.zeros_like(lb_ref)
            lc_ref[...] = before_refs[1][...] if before else jnp.zeros_like(lc_ref)

        for h, head_ref in enumerate((own_ref, sib_ref)):
            out = slice(h * vocab, (h + 1) * vocab)

            def over_x(ref):
                return sum(
                    lax.dot_general(
                        ref[:, i * f : (i + 1) * f],
                        head_ref[:, along_x(order_ref, i, f)],
                        NT,
                        preferred_element_type=F32,
                    )
                    for i in range(SIDE)
                )

            la_ref[:, out] += over_x(a_ref)
            lb_ref[:, out] += lax.dot_general(
                b_ref[...], head_ref[:, along_x(order_ref, q, f)], NT, preferred_element_type=F32
            )

            @pl.when(k == q)
            def _():
                lc_ref[:, out] += over_x(c_ref)

        if last:
            stats_ref, rows_ref = refs

            @pl.when(k == SIDE - 1)
            def _():
                for p in range(SIDE):
                    offset = 0
                    for ref, meta_ref, n in (
                        (la_ref if p == SIDE - 1 else earlier_refs[0], meta_refs[0], ra),
                        (lb_ref, meta_refs[1], rb // SIDE),
                        (lc_ref, meta_refs[2], rc // SIDE),
                    ):
                        rows = slice(0, n) if ref.shape[0] == n else slice(p * n, (p + 1) * n)
                        lse, pick = statistics(ref[rows, :], meta_ref[p * n : (p + 1) * n, :])
                        lane = lax.broadcasted_iota(jnp.int32, (n, 128), 1)
                        rows_ref[p * tok + offset : p * tok + offset + n, :] = jnp.where(
                            lane < 1, lse, pick
                        )
                        offset += n
                stats_ref[...] = rows_ref[...].T[:8, :]

    two = 2 * vocab
    in_specs = [column((ra, side)), column((rb, f)), whole(xc.shape)]
    in_specs += [slab((vocab, side))] * 2
    extra = list(before) + list(metas or ()) + list(earlier)
    in_specs += [whole(e.shape) for e in extra]
    shapes = [(ra, two), (rb, two), (rc, two)] + ([(8, SIDE * tok)] if last else [])
    return pl.pallas_call(
        kernel,
        out_shape=[jax.ShapeDtypeStruct(shape, F32) for shape in shapes],
        grid_spec=pltpu.PrefetchScalarGridSpec(
            num_scalar_prefetch=1,
            grid=(SIDE,),
            in_specs=in_specs,
            out_specs=[whole(shape) for shape in shapes],
            scratch_shapes=[pltpu.VMEM((SIDE * tok, 128), F32)] if last else [],
        ),
        compiler_params=params(),
        cost_estimate=cost(
            4 * vocab * (ra * width + (rb + rc) * side), 4 * vocab * width + 4 * ra * width
        ),
    )(order, xa, xb, xc, own, sib, *extra)


def cross_specs(q, vocab, f):
    over_y = pl.BlockSpec((vocab, f), lambda k, order: (0, order[k] * SIDE + order[SIDE + q]))
    over_x = pl.BlockSpec((vocab, f), lambda k, order: (0, order[q] * SIDE + order[SIDE + k]))
    return [over_y, over_x, over_y, over_x]


def logits_cross(q, xb, xc, own, sib, order, before):
    rb, rc = xb.shape[0], xc.shape[0]
    vocab, width = own.shape
    f = width // (SIDE * SIDE)
    two = 2 * vocab

    def kernel(order_ref, b_ref, c_ref, own_y, own_x, sib_y, sib_x, *refs):
        lb_ref, lc_ref = refs[-2:]

        @pl.when(pl.program_id(0) == 0)
        def _():
            lb_ref[...] = refs[0][...] if before else jnp.zeros_like(lb_ref)
            lc_ref[...] = refs[1][...] if before else jnp.zeros_like(lc_ref)

        for out, y_ref, x_ref in (
            (slice(0, vocab), own_y, own_x),
            (slice(vocab, two), sib_y, sib_x),
        ):
            lb_ref[:, out] += lax.dot_general(
                b_ref[...], y_ref[...], NT, preferred_element_type=F32
            )
            lc_ref[:, out] += lax.dot_general(
                c_ref[...], x_ref[...], NT, preferred_element_type=F32
            )

    return pl.pallas_call(
        kernel,
        out_shape=[jax.ShapeDtypeStruct((r, two), F32) for r in (rb, rc)],
        grid_spec=pltpu.PrefetchScalarGridSpec(
            num_scalar_prefetch=1,
            grid=(SIDE,),
            in_specs=[column((rb, f)), column((rc, f))]
            + cross_specs(q, vocab, f)
            + [whole(e.shape) for e in before],
            out_specs=[whole((r, two)) for r in (rb, rc)],
        ),
        compiler_params=params(),
        cost_estimate=cost(4 * vocab * (rb + rc) * SIDE * f, 20 * vocab * SIDE * f),
    )(order, xb, xc, own, own, sib, sib, *before)


def terms_cross(q, db, dc, own, sib, order):
    rb, rc = db.shape[0], dc.shape[0]
    vocab, width = own.shape
    f = width // (SIDE * SIDE)

    def kernel(order_ref, db_ref, dc_ref, own_y, own_x, sib_y, sib_x, tb_ref, tc_ref):
        for d_ref, o_ref, s_ref, out_ref in (
            (db_ref, own_y, sib_y, tb_ref),
            (dc_ref, own_x, sib_x, tc_ref),
        ):
            total = jnp.dot(d_ref[:, :vocab], o_ref[...], preferred_element_type=F32)
            total += jnp.dot(d_ref[:, vocab:], s_ref[...], preferred_element_type=F32)
            out_ref[...] = total.astype(BF16)

    return pl.pallas_call(
        kernel,
        out_shape=[jax.ShapeDtypeStruct((r, SIDE * f), BF16) for r in (rb, rc)],
        grid_spec=pltpu.PrefetchScalarGridSpec(
            num_scalar_prefetch=1,
            grid=(SIDE,),
            in_specs=[whole(db.shape), whole(dc.shape)] + cross_specs(q, vocab, f),
            out_specs=[column((rb, f)), column((rc, f))],
        ),
        compiler_params=params(),
        cost_estimate=cost(4 * vocab * (rb + rc) * SIDE * f, 20 * vocab * SIDE * f),
    )(order, db, dc, own, own, sib, sib)


def dlogits(everyone, la, lb, lc, metas, order):
    two = lb.shape[1]
    vocab = two // 2
    sizes = (la[1].shape[0], lb.shape[0] // SIDE, lc.shape[0] // SIDE)
    tok = sum(sizes)
    every = SIDE * tok
    square = SIDE * SIDE

    def kernel(order_ref, all_ref, *refs):
        early_ref, late_ref, lb_ref, lc_ref = refs[:4]
        meta_refs = refs[4:7]
        loss_ref, da_ref, db_ref, dc_ref, rows_ref, wide_ref = refs[7:]
        parts, weights = [], []
        for r in range(SIDE):
            start = pl.multiple_of(order_ref[2 * SIDE + r] * square, square)
            block = all_ref[pl.ds(start, square), :every]
            if r:
                cut = (SIDE - r) * tok
                block = jnp.concatenate([block[:, cut:], block[:, :cut]], 1)
            parts.append(block)
            weights.append(all_ref[pl.ds(start, 8), every + tok : every + 2 * tok][:1, :])
        parts = jnp.concatenate(parts, 0)
        top = jnp.max(parts, axis=0, keepdims=True)
        lse = top + jnp.log(jnp.sum(jnp.exp(parts - top), axis=0, keepdims=True))
        pick = jnp.sum(all_ref[:, every : every + tok], axis=0, keepdims=True)
        loss_ref[...] = lse[:, :tok] - pick
        weight = jnp.concatenate(weights, 1)
        sub = lax.broadcasted_iota(jnp.int32, (128, every), 0)
        rows_ref[...] = jnp.where(sub < 64, lse, weight).T
        offset = 0
        for i, (n, out_ref) in enumerate(zip(sizes, (da_ref, db_ref, dc_ref))):
            for p in range(SIDE):
                own = slice(p * n, (p + 1) * n)
                at = slice(p * tok + offset, p * tok + offset + n)
                if i == 0:
                    value = late_ref[...] if p == SIDE - 1 else early_ref[own, :]
                else:
                    value = (lb_ref, lc_ref)[i - 1][own, :]
                local = lax.broadcasted_iota(jnp.int32, (n, vocab), 1)
                for h in range(2):
                    cols = slice(h * vocab, (h + 1) * vocab)
                    has = meta_refs[i][own, h : h + 1] > 0
                    hit = (local == meta_refs[i][own, 2 + h : 3 + h]).astype(F32)
                    wide_ref[own, cols] = jnp.where(
                        has,
                        rows_ref[at, 64:65]
                        * (jnp.exp(value[:, cols] - rows_ref[at, 0:1]) - hit),
                        0.0,
                    )
            offset += n
            out_ref[...] = wide_ref[: SIDE * n, :].astype(BF16)

    args = [everyone, *la, lb, lc, *metas]
    shapes = [(1, tok)] + [(SIDE * n, two) for n in sizes]
    types = [F32, BF16, BF16, BF16]
    return pl.pallas_call(
        kernel,
        out_shape=[jax.ShapeDtypeStruct(s, t) for s, t in zip(shapes, types)],
        grid_spec=pltpu.PrefetchScalarGridSpec(
            num_scalar_prefetch=1,
            grid=(1,),
            in_specs=[whole(a.shape) for a in args],
            out_specs=[whole(s) for s in shapes],
            scratch_shapes=[
                pltpu.VMEM((every, 128), F32),
                pltpu.VMEM((SIDE * max(sizes), two), F32),
            ],
        ),
        compiler_params=params(),
        cost_estimate=cost(20 * every * two, 6 * every * two),
    )(order, *args)


def terms_tick(q, dls, own, sib, order):
    ra, rb, rc = (d.shape[0] for d in dls)
    vocab, width = own.shape
    f = width // (SIDE * SIDE)
    side = f * SIDE

    def kernel(order_ref, da_ref, db_ref, dc_ref, own_ref, sib_ref, ta_ref, tb_ref, tc_ref):
        def times(ref, i):
            cols = along_x(order_ref, i, f)
            total = jnp.dot(ref[:, :vocab], own_ref[:, cols], preferred_element_type=F32)
            total += jnp.dot(ref[:, vocab:], sib_ref[:, cols], preferred_element_type=F32)
            return total.astype(BF16)

        for i in range(SIDE):
            ta_ref[:, i * f : (i + 1) * f] = times(da_ref, i)
        tb_ref[...] = times(db_ref, q)

        @pl.when(pl.program_id(0) == q)
        def _():
            for i in range(SIDE):
                tc_ref[:, i * f : (i + 1) * f] = times(dc_ref, i)

    return pl.pallas_call(
        kernel,
        out_shape=[
            jax.ShapeDtypeStruct((ra, width), BF16),
            jax.ShapeDtypeStruct((rb, side), BF16),
            jax.ShapeDtypeStruct((rc, side), BF16),
        ],
        grid_spec=pltpu.PrefetchScalarGridSpec(
            num_scalar_prefetch=1,
            grid=(SIDE,),
            in_specs=[whole(d.shape) for d in dls] + [slab((vocab, side))] * 2,
            out_specs=[column((ra, side)), column((rb, f)), whole((rc, side))],
        ),
        compiler_params=params(),
        cost_estimate=cost(
            4 * vocab * (ra * width + (rb + rc) * side), 4 * vocab * width + 4 * ra * width
        ),
    )(order, *dls, own, sib)


def head_part(dlt, xa, xb, xc, order, before=None):
    vocab, rows = dlt.shape
    ra, width = xa.shape
    rb, rc = xb[0].shape[0], xc[0].shape[0]
    f = width // (SIDE * SIDE)
    side = f * SIDE

    def kernel(order_ref, d_ref, a_ref, *refs):
        b_refs, c_refs = refs[:SIDE], refs[SIDE : 2 * SIDE]
        out_ref, x_ref = refs[-2:]
        x_ref[:ra, :] = a_ref[...]
        for i in range(SIDE):
            x_ref[ra : ra + rb, i * f : (i + 1) * f] = b_refs[i][...]

            @pl.when(pl.program_id(0) == i)
            def _():
                x_ref[ra + rb :, :] = c_refs[i][...]

        for i in range(SIDE):
            cols = along_x(order_ref, i, f)
            total = jnp.dot(
                d_ref[...], x_ref[:, i * f : (i + 1) * f], preferred_element_type=F32
            )
            if before is not None:
                total += refs[2 * SIDE][:, cols].astype(F32)
            out_ref[:, cols] = total.astype(BF16)

    in_specs = [whole(dlt.shape), column((ra, side))]
    in_specs += [column((rb, f))] * SIDE + [whole(v.shape) for v in xc]
    args = [dlt, xa, *xb, *xc]
    if before is not None:
        in_specs.append(slab((vocab, side)))
        args.append(before)
    return pl.pallas_call(
        kernel,
        out_shape=jax.ShapeDtypeStruct((vocab, width), BF16),
        grid_spec=pltpu.PrefetchScalarGridSpec(
            num_scalar_prefetch=1,
            grid=(SIDE,),
            in_specs=in_specs,
            out_specs=slab((vocab, side)),
            scratch_shapes=[pltpu.VMEM((rows, side), BF16)],
        ),
        compiler_params=params(),
        cost_estimate=cost(2 * rows * vocab * width, 2 * (rows + vocab) * width),
    )(order, *args)


def on_device(hidden, head, block_lists, target_slot, loss_grad):
    z, c, y, x = (lax.axis_index(a) for a in AXES)
    sign = 1 - 2 * c
    tok, f = hidden.shape
    vocab, width = head.shape
    tb_row = tok // BLK
    groups = SIDE * CORES
    first = 11 * tok // 256 * 8
    second = first
    cuts = (0, first, first + second, tok)
    quarter = jnp.arange(SIDE, dtype=jnp.int32)
    at_z = (z - sign * quarter) % SIDE
    at_y = (y - sign * quarter) % SIDE
    at_x = (x - sign * quarter) % SIDE
    order = jnp.concatenate([at_y, at_x, at_z])

    sib = swap_cores(head)

    def by_part(rows_of_dp):
        return [rows_of_dp[:, a:b].reshape(-1) for a, b in zip(cuts[:-1], cuts[1:])]

    dp_at = at_z * CORES + c
    lists = pick_rows(block_lists.reshape(groups, tb_row, -1), dp_at)
    slots = pick_rows(target_slot.reshape(groups, tb_row, BLK), dp_at)
    wanted = jnp.sum(
        jnp.where(
            (slots // vocab)[..., None] == jnp.arange(lists.shape[2], dtype=jnp.int32),
            lists[:, :, None, :],
            0,
        ),
        axis=3,
    )
    base = (y * SIDE + x) * groups + z * CORES
    kinds = []
    for block in (base + c, base + 1 - c):
        named = jnp.any(lists == block, axis=2)
        kinds.append(jnp.broadcast_to(named[:, :, None], slots.shape).astype(jnp.int32))
    for block in (base + c, base + 1 - c):
        kinds.append(jnp.where(wanted == block, slots % vocab, -1))
    kinds = [by_part(kind.reshape(SIDE, tok)) for kind in kinds]
    metas = [jnp.stack([kind[i] for kind in kinds], 1) for i in range(3)]

    parts = [hidden[a:b] for a, b in zip(cuts[:-1], cuts[1:])]
    parts = gather_ring(parts, "xyz", (1, 1, 0))
    parts = gather_ring(parts, "yzx", (1, 0, 1))
    chunks = [[p] for p in parts]
    sums = ()
    for q in range(SIDE - 1):
        if q < SIDE - 2:
            beside = logits_cross(q, chunks[1][q], chunks[2][q], head, sib, order, sums)
            sums = ring_tick(chunks, "zxy", beside)
        else:
            now = [jnp.concatenate(chunks[0], 0), chunks[1][q], chunks[2][q]]
            beside = logits_tick(q, now, head, sib, order, sums)
            early, *sums = ring_tick(chunks, "zxy", beside)
    now = [p[-1] for p in chunks]
    late, lb, lc, stats = logits_tick(SIDE - 1, now, head, sib, order, sums, metas, [early])
    la = [early, late]

    to_q = (sign * (z - quarter)) % SIDE
    pick = pick_rows(stats[1].reshape(SIDE, tok), to_q)
    square, count = SIDE**2, SIDE**3
    flat = jnp.concatenate(
        [
            jnp.broadcast_to(stats[0][None], (count, SIDE * tok)),
            jnp.broadcast_to(pick[:, None], (SIDE, square, tok)).reshape(count, tok),
            jnp.broadcast_to(loss_grad[None], (count, tok)),
        ],
        1,
    )
    everyone = lax.all_to_all(flat, ("z", "y", "x"), 0, 0, tiled=True)
    losses, *dls = dlogits(everyone, la, lb, lc, metas, order)
    losses = losses.reshape(tok)

    n = dls[0].shape[0] // SIDE
    rest = jnp.concatenate([dls[0][2 * n :], dls[0][:n]], 0)
    sums = terms_tick(1, [dls[0][n : 2 * n], dls[1], dls[2]], head, sib, order)
    for q in (2, 3, 0):
        moved = [shift(s, axis, 1) for s, axis in zip(sums, "zxy")]
        if q == 2:
            others, *terms = terms_tick(2, [rest, dls[1], dls[2]], head, sib, order)
            others = jnp.split(others, SIDE - 1, 0)
            moved, dls, last = bar((moved, dls, chunks[0]))
            dlt = jnp.concatenate(dls, 0).T
            xs = jnp.concatenate(last, 0), chunks[1], chunks[2]
        else:
            terms = terms_cross(q, dls[1], dls[2], head, sib, order)
        if q == 3:
            theirs = head_part(dlt[vocab:], *xs, order)
            moved, theirs = bar((moved, theirs))
        terms = [others[(q - 2) % SIDE], *terms]
        sums = [(m.astype(F32) + t.astype(F32)).astype(BF16) for m, t in zip(moved, terms)]
    head_grad = head_part(dlt[:vocab], *xs, order, swap_cores(theirs))
    sums, head_grad = scatter_direct(sums, "yzx", (1, 0, 1), head_grad)
    sums, _ = scatter_direct(sums, "xyz", (1, 1, 0))
    hidden_grad = jnp.concatenate(sums, 0)
    return losses, hidden_grad, head_grad


def solution(mesh):
    grid = Mesh(mesh.devices.reshape(SIDE, CORES, SIDE, SIDE), AXES)
    dp, owners = ("z", "c"), ("y", "x")
    in_specs = (P(dp, owners), P(owners + dp, None), P(), P(), P(dp))
    out_specs = (P(dp), P(dp, owners), P(owners + dp, None))
    return jax.shard_map(
        on_device, mesh=grid, in_specs=in_specs, out_specs=out_specs, check_vma=False
    )
```

```python
import jax
import jax.numpy as jnp
from jax import lax
from jax.experimental import pallas as pl
from jax.experimental.pallas import tpu as pltpu
from jax.sharding import Mesh
from jax.sharding import PartitionSpec as P

BLK = 128
SIDE = 4
CORES = 2
AXES = ("z", "c", "y", "x")
LOW = -1e30
VMEM_LIMIT = 48 * 2**20
F32 = jnp.float32
BF16 = jnp.bfloat16
bar = lax.optimization_barrier


def signed_pairs(axis, steps):
    pairs = []
    for z in range(SIDE):
        for c in range(CORES):
            for y in range(SIDE):
                for x in range(SIDE):
                    at = {"z": z, "y": y, "x": x}
                    to = dict(at)
                    to[axis] = (at[axis] + (1 - 2 * c) * steps) % SIDE

                    def line(p):
                        return ((p["z"] * CORES + c) * SIDE + p["y"]) * SIDE + p["x"]

                    pairs.append((line(at), line(to)))
    return pairs


def shift(array, axis, steps):
    return lax.ppermute(array, AXES, signed_pairs(axis, steps))


def pick_rows(array, at):
    return jnp.stack(
        [lax.dynamic_index_in_dim(array, at[q], 0, keepdims=False) for q in range(SIDE)]
    )


def swap_cores(array):
    return lax.ppermute(array, "c", [(0, 1), (1, 0)])


def ring_tick(chunks, axes, beside=()):
    moved = [shift(p[-1], axis, 1) for p, axis in zip(chunks, axes)]
    moved, beside = bar((moved, beside))
    for p, m in zip(chunks, moved):
        p.append(m)
    return beside


def gather_ring(arrays, axes, dims):
    chunks = [[a] for a in arrays]
    for step in range(SIDE - 1):
        ring_tick(chunks, axes)
    return list(bar([jnp.concatenate(p, dim) for p, dim in zip(chunks, dims)]))


def scatter_direct(arrays, axes, dims, beside=()):
    parts = [jnp.split(a, SIDE, dim) for a, dim in zip(arrays, dims)]
    moved = [
        [shift(p[q], axis, -q) for q in range(1, SIDE)] for p, axis in zip(parts, axes)
    ]
    moved, beside = bar((moved, beside))
    sums = [
        (p[0].astype(F32) + m[0].astype(F32) + m[1].astype(F32) + m[2].astype(F32)).astype(BF16)
        for p, m in zip(parts, moved)
    ]
    return sums, beside


def params():
    return pltpu.CompilerParams(vmem_limit_bytes=VMEM_LIMIT)


def cost(flops, bytes_accessed):
    return pl.CostEstimate(flops=flops, bytes_accessed=bytes_accessed, transcendentals=0)


NT = (((1,), (1,)), ((), ()))


def whole(shape):
    return pl.BlockSpec(shape, lambda k, order: (0,) * len(shape))


def slab(shape):
    return pl.BlockSpec(shape, lambda k, order: (0, order[k]))


def column(shape):
    return pl.BlockSpec(shape, lambda k, order: (0, k))


def along_x(order, q, f):
    return pl.ds(pl.multiple_of(order[SIDE + q] * f, f), f)


def statistics(logits, meta):
    vocab = logits.shape[1] // 2
    local = lax.broadcasted_iota(jnp.int32, (logits.shape[0], vocab), 1)
    halves = (logits[:, :vocab], logits[:, vocab:])
    has = [meta[:, h : h + 1] > 0 for h in range(2)]
    tops = [
        jnp.where(n, jnp.max(l, axis=1, keepdims=True), LOW) for n, l in zip(has, halves)
    ]
    top = jnp.maximum(tops[0], tops[1])
    total = pick = 0.0
    for h in range(2):
        total += jnp.where(
            has[h], jnp.sum(jnp.exp(halves[h] - top), axis=1, keepdims=True), 0.0
        )
        pick += jnp.sum(
            jnp.where(local == meta[:, 2 + h : 3 + h], halves[h], 0.0), axis=1, keepdims=True
        )
    found = total > 0
    lse = jnp.where(found, top + jnp.log(jnp.where(found, total, 1.0)), LOW)
    return lse, pick


def logits_tick(q, chunks, own, sib, order, before, metas=None, earlier=()):
    xa, xb, xc = chunks
    ra, rb, rc = (v.shape[0] for v in chunks)
    vocab, width = own.shape
    f = width // (SIDE * SIDE)
    side = f * SIDE
    last = metas is not None
    tok = ra + (rb + rc) // SIDE

    def kernel(order_ref, *refs):
        refs = list(refs)
        a_ref, b_ref, c_ref, own_ref, sib_ref = (refs.pop(0) for _ in range(5))
        before_refs = [refs.pop(0) for _ in before]
        meta_refs = [refs.pop(0) for _ in (metas or ())]
        earlier_refs = [refs.pop(0) for _ in earlier]
        la_ref, lb_ref, lc_ref = (refs.pop(0) for _ in range(3))
        k = pl.program_id(0)

        @pl.when(k == 0)
        def _():
            la_ref[...] = jnp.zeros_like(la_ref)
            lb_ref[...] = before_refs[0][...] if before else jnp.zeros_like(lb_ref)
            lc_ref[...] = before_refs[1][...] if before else jnp.zeros_like(lc_ref)

        for h, head_ref in enumerate((own_ref, sib_ref)):
            out = slice(h * vocab, (h + 1) * vocab)

            def over_x(ref):
                return sum(
                    lax.dot_general(
                        ref[:, i * f : (i + 1) * f],
                        head_ref[:, along_x(order_ref, i, f)],
                        NT,
                        preferred_element_type=F32,
                    )
                    for i in range(SIDE)
                )

            la_ref[:, out] += over_x(a_ref)
            lb_ref[:, out] += lax.dot_general(
                b_ref[...], head_ref[:, along_x(order_ref, q, f)], NT, preferred_element_type=F32
            )

            @pl.when(k == q)
            def _():
                lc_ref[:, out] += over_x(c_ref)

        if last:
            stats_ref, rows_ref = refs

            @pl.when(k == SIDE - 1)
            def _():
                for p in range(SIDE):
                    offset = 0
                    for ref, meta_ref, n in (
                        (la_ref if p == SIDE - 1 else earlier_refs[0], meta_refs[0], ra),
                        (lb_ref, meta_refs[1], rb // SIDE),
                        (lc_ref, meta_refs[2], rc // SIDE),
                    ):
                        rows = slice(0, n) if ref.shape[0] == n else slice(p * n, (p + 1) * n)
                        lse, pick = statistics(ref[rows, :], meta_ref[p * n : (p + 1) * n, :])
                        lane = lax.broadcasted_iota(jnp.int32, (n, 128), 1)
                        rows_ref[p * tok + offset : p * tok + offset + n, :] = jnp.where(
                            lane < 1, lse, pick
                        )
                        offset += n
                stats_ref[...] = rows_ref[...].T[:8, :]

    two = 2 * vocab
    in_specs = [column((ra, side)), column((rb, f)), whole(xc.shape)]
    in_specs += [slab((vocab, side))] * 2
    extra = list(before) + list(metas or ()) + list(earlier)
    in_specs += [whole(e.shape) for e in extra]
    shapes = [(ra, two), (rb, two), (rc, two)] + ([(8, SIDE * tok)] if last else [])
    return pl.pallas_call(
        kernel,
        out_shape=[jax.ShapeDtypeStruct(shape, F32) for shape in shapes],
        grid_spec=pltpu.PrefetchScalarGridSpec(
            num_scalar_prefetch=1,
            grid=(SIDE,),
            in_specs=in_specs,
            out_specs=[whole(shape) for shape in shapes],
            scratch_shapes=[pltpu.VMEM((SIDE * tok, 128), F32)] if last else [],
        ),
        compiler_params=params(),
        cost_estimate=cost(
            4 * vocab * (ra * width + (rb + rc) * side), 4 * vocab * width + 4 * ra * width
        ),
    )(order, xa, xb, xc, own, sib, *extra)


def cross_specs(q, vocab, f):
    over_y = pl.BlockSpec((vocab, f), lambda k, order: (0, order[k] * SIDE + order[SIDE + q]))
    over_x = pl.BlockSpec((vocab, f), lambda k, order: (0, order[q] * SIDE + order[SIDE + k]))
    return [over_y, over_x, over_y, over_x]


def logits_cross(q, xb, xc, own, sib, order, before):
    rb, rc = xb.shape[0], xc.shape[0]
    vocab, width = own.shape
    f = width // (SIDE * SIDE)
    two = 2 * vocab

    def kernel(order_ref, b_ref, c_ref, own_y, own_x, sib_y, sib_x, *refs):
        lb_ref, lc_ref = refs[-2:]

        @pl.when(pl.program_id(0) == 0)
        def _():
            lb_ref[...] = refs[0][...] if before else jnp.zeros_like(lb_ref)
            lc_ref[...] = refs[1][...] if before else jnp.zeros_like(lc_ref)

        for out, y_ref, x_ref in (
            (slice(0, vocab), own_y, own_x),
            (slice(vocab, two), sib_y, sib_x),
        ):
            lb_ref[:, out] += lax.dot_general(
                b_ref[...], y_ref[...], NT, preferred_element_type=F32
            )
            lc_ref[:, out] += lax.dot_general(
                c_ref[...], x_ref[...], NT, preferred_element_type=F32
            )

    return pl.pallas_call(
        kernel,
        out_shape=[jax.ShapeDtypeStruct((r, two), F32) for r in (rb, rc)],
        grid_spec=pltpu.PrefetchScalarGridSpec(
            num_scalar_prefetch=1,
            grid=(SIDE,),
            in_specs=[column((rb, f)), column((rc, f))]
            + cross_specs(q, vocab, f)
            + [whole(e.shape) for e in before],
            out_specs=[whole((r, two)) for r in (rb, rc)],
        ),
        compiler_params=params(),
        cost_estimate=cost(4 * vocab * (rb + rc) * SIDE * f, 20 * vocab * SIDE * f),
    )(order, xb, xc, own, own, sib, sib, *before)


def terms_cross(q, db, dc, own, sib, order):
    rb, rc = db.shape[0], dc.shape[0]
    vocab, width = own.shape
    f = width // (SIDE * SIDE)

    def kernel(order_ref, db_ref, dc_ref, own_y, own_x, sib_y, sib_x, tb_ref, tc_ref):
        for d_ref, o_ref, s_ref, out_ref in (
            (db_ref, own_y, sib_y, tb_ref),
            (dc_ref, own_x, sib_x, tc_ref),
        ):
            total = jnp.dot(d_ref[:, :vocab], o_ref[...], preferred_element_type=F32)
            total += jnp.dot(d_ref[:, vocab:], s_ref[...], preferred_element_type=F32)
            out_ref[...] = total.astype(BF16)

    return pl.pallas_call(
        kernel,
        out_shape=[jax.ShapeDtypeStruct((r, SIDE * f), BF16) for r in (rb, rc)],
        grid_spec=pltpu.PrefetchScalarGridSpec(
            num_scalar_prefetch=1,
            grid=(SIDE,),
            in_specs=[whole(db.shape), whole(dc.shape)] + cross_specs(q, vocab, f),
            out_specs=[column((rb, f)), column((rc, f))],
        ),
        compiler_params=params(),
        cost_estimate=cost(4 * vocab * (rb + rc) * SIDE * f, 20 * vocab * SIDE * f),
    )(order, db, dc, own, own, sib, sib)


def dlogits(everyone, la, lb, lc, metas, order):
    two = lb.shape[1]
    vocab = two // 2
    sizes = (la[1].shape[0], lb.shape[0] // SIDE, lc.shape[0] // SIDE)
    tok = sum(sizes)
    every = SIDE * tok
    square = SIDE * SIDE

    def kernel(order_ref, all_ref, *refs):
        early_ref, late_ref, lb_ref, lc_ref = refs[:4]
        meta_refs = refs[4:7]
        loss_ref, da_ref, db_ref, dc_ref, rows_ref, wide_ref = refs[7:]
        parts, weights = [], []
        for r in range(SIDE):
            start = pl.multiple_of(order_ref[2 * SIDE + r] * square, square)
            block = all_ref[pl.ds(start, square), :every]
            if r:
                cut = (SIDE - r) * tok
                block = jnp.concatenate([block[:, cut:], block[:, :cut]], 1)
            parts.append(block)
            weights.append(all_ref[pl.ds(start, 8), every + tok : every + 2 * tok][:1, :])
        parts = jnp.concatenate(parts, 0)
        top = jnp.max(parts, axis=0, keepdims=True)
        lse = top + jnp.log(jnp.sum(jnp.exp(parts - top), axis=0, keepdims=True))
        pick = jnp.sum(all_ref[:, every : every + tok], axis=0, keepdims=True)
        loss_ref[...] = lse[:, :tok] - pick
        weight = jnp.concatenate(weights, 1)
        sub = lax.broadcasted_iota(jnp.int32, (128, every), 0)
        rows_ref[...] = jnp.where(sub < 64, lse, weight).T
        offset = 0
        for i, (n, out_ref) in enumerate(zip(sizes, (da_ref, db_ref, dc_ref))):
            for p in range(SIDE):
                own = slice(p * n, (p + 1) * n)
                at = slice(p * tok + offset, p * tok + offset + n)
                if i == 0:
                    value = late_ref[...] if p == SIDE - 1 else early_ref[own, :]
                else:
                    value = (lb_ref, lc_ref)[i - 1][own, :]
                local = lax.broadcasted_iota(jnp.int32, (n, vocab), 1)
                for h in range(2):
                    cols = slice(h * vocab, (h + 1) * vocab)
                    has = meta_refs[i][own, h : h + 1] > 0
                    hit = (local == meta_refs[i][own, 2 + h : 3 + h]).astype(F32)
                    wide_ref[own, cols] = jnp.where(
                        has,
                        rows_ref[at, 64:65]
                        * (jnp.exp(value[:, cols] - rows_ref[at, 0:1]) - hit),
                        0.0,
                    )
            offset += n
            out_ref[...] = wide_ref[: SIDE * n, :].astype(BF16)

    args = [everyone, *la, lb, lc, *metas]
    shapes = [(1, tok)] + [(SIDE * n, two) for n in sizes]
    types = [F32, BF16, BF16, BF16]
    return pl.pallas_call(
        kernel,
        out_shape=[jax.ShapeDtypeStruct(s, t) for s, t in zip(shapes, types)],
        grid_spec=pltpu.PrefetchScalarGridSpec(
            num_scalar_prefetch=1,
            grid=(1,),
            in_specs=[whole(a.shape) for a in args],
            out_specs=[whole(s) for s in shapes],
            scratch_shapes=[
                pltpu.VMEM((every, 128), F32),
                pltpu.VMEM((SIDE * max(sizes), two), F32),
            ],
        ),
        compiler_params=params(),
        cost_estimate=cost(20 * every * two, 6 * every * two),
    )(order, *args)


def terms_tick(q, dls, own, sib, order):
    ra, rb, rc = (d.shape[0] for d in dls)
    vocab, width = own.shape
    f = width // (SIDE * SIDE)
    side = f * SIDE

    def kernel(order_ref, da_ref, db_ref, dc_ref, own_ref, sib_ref, ta_ref, tb_ref, tc_ref):
        def times(ref, i):
            cols = along_x(order_ref, i, f)
            total = jnp.dot(ref[:, :vocab], own_ref[:, cols], preferred_element_type=F32)
            total += jnp.dot(ref[:, vocab:], sib_ref[:, cols], preferred_element_type=F32)
            return total.astype(BF16)

        for i in range(SIDE):
            ta_ref[:, i * f : (i + 1) * f] = times(da_ref, i)
        tb_ref[...] = times(db_ref, q)

        @pl.when(pl.program_id(0) == q)
        def _():
            for i in range(SIDE):
                tc_ref[:, i * f : (i + 1) * f] = times(dc_ref, i)

    return pl.pallas_call(
        kernel,
        out_shape=[
            jax.ShapeDtypeStruct((ra, width), BF16),
            jax.ShapeDtypeStruct((rb, side), BF16),
            jax.ShapeDtypeStruct((rc, side), BF16),
        ],
        grid_spec=pltpu.PrefetchScalarGridSpec(
            num_scalar_prefetch=1,
            grid=(SIDE,),
            in_specs=[whole(d.shape) for d in dls] + [slab((vocab, side))] * 2,
            out_specs=[column((ra, side)), column((rb, f)), whole((rc, side))],
        ),
        compiler_params=params(),
        cost_estimate=cost(
            4 * vocab * (ra * width + (rb + rc) * side), 4 * vocab * width + 4 * ra * width
        ),
    )(order, *dls, own, sib)


def head_part(dlt, xa, xb, xc, order, before=None):
    vocab, rows = dlt.shape
    ra, width = xa.shape
    rb, rc = xb[0].shape[0], xc[0].shape[0]
    f = width // (SIDE * SIDE)
    side = f * SIDE

    def kernel(order_ref, d_ref, a_ref, *refs):
        b_refs, c_refs = refs[:SIDE], refs[SIDE : 2 * SIDE]
        out_ref, x_ref = refs[-2:]
        x_ref[:ra, :] = a_ref[...]
        for i in range(SIDE):
            x_ref[ra : ra + rb, i * f : (i + 1) * f] = b_refs[i][...]

            @pl.when(pl.program_id(0) == i)
            def _():
                x_ref[ra + rb :, :] = c_refs[i][...]

        for i in range(SIDE):
            cols = along_x(order_ref, i, f)
            total = jnp.dot(
                d_ref[...], x_ref[:, i * f : (i + 1) * f], preferred_element_type=F32
            )
            if before is not None:
                total += refs[2 * SIDE][:, cols].astype(F32)
            out_ref[:, cols] = total.astype(BF16)

    in_specs = [whole(dlt.shape), column((ra, side))]
    in_specs += [column((rb, f))] * SIDE + [whole(v.shape) for v in xc]
    args = [dlt, xa, *xb, *xc]
    if before is not None:
        in_specs.append(slab((vocab, side)))
        args.append(before)
    return pl.pallas_call(
        kernel,
        out_shape=jax.ShapeDtypeStruct((vocab, width), BF16),
        grid_spec=pltpu.PrefetchScalarGridSpec(
            num_scalar_prefetch=1,
            grid=(SIDE,),
            in_specs=in_specs,
            out_specs=slab((vocab, side)),
            scratch_shapes=[pltpu.VMEM((rows, side), BF16)],
        ),
        compiler_params=params(),
        cost_estimate=cost(2 * rows * vocab * width, 2 * (rows + vocab) * width),
    )(order, *args)


def on_device(hidden, head, block_lists, target_slot, loss_grad):
    z, c, y, x = (lax.axis_index(a) for a in AXES)
    sign = 1 - 2 * c
    tok, f = hidden.shape
    vocab, width = head.shape
    tb_row = tok // BLK
    groups = SIDE * CORES
    first = 11 * tok // 256 * 8
    second = first
    cuts = (0, first, first + second, tok)
    quarter = jnp.arange(SIDE, dtype=jnp.int32)
    at_z = (z - sign * quarter) % SIDE
    at_y = (y - sign * quarter) % SIDE
    at_x = (x - sign * quarter) % SIDE
    order = jnp.concatenate([at_y, at_x, at_z])

    sib = swap_cores(head)

    def by_part(rows_of_dp):
        return [rows_of_dp[:, a:b].reshape(-1) for a, b in zip(cuts[:-1], cuts[1:])]

    dp_at = at_z * CORES + c
    lists = pick_rows(block_lists.reshape(groups, tb_row, -1), dp_at)
    slots = pick_rows(target_slot.reshape(groups, tb_row, BLK), dp_at)
    wanted = jnp.sum(
        jnp.where(
            (slots // vocab)[..., None] == jnp.arange(lists.shape[2], dtype=jnp.int32),
            lists[:, :, None, :],
            0,
        ),
        axis=3,
    )
    base = (y * SIDE + x) * groups + z * CORES
    kinds = []
    for block in (base + c, base + 1 - c):
        named = jnp.any(lists == block, axis=2)
        kinds.append(jnp.broadcast_to(named[:, :, None], slots.shape).astype(jnp.int32))
    for block in (base + c, base + 1 - c):
        kinds.append(jnp.where(wanted == block, slots % vocab, -1))
    kinds = [by_part(kind.reshape(SIDE, tok)) for kind in kinds]
    metas = [jnp.stack([kind[i] for kind in kinds], 1) for i in range(3)]

    parts = [hidden[a:b] for a, b in zip(cuts[:-1], cuts[1:])]
    parts = gather_ring(parts, "xyz", (1, 1, 0))
    parts = gather_ring(parts, "yzx", (1, 0, 1))
    chunks = [[p] for p in parts]
    sums = ()
    for q in range(SIDE - 1):
        if q < SIDE - 2:
            beside = logits_cross(q, chunks[1][q], chunks[2][q], head, sib, order, sums)
            sums = ring_tick(chunks, "zxy", beside)
        else:
            now = [jnp.concatenate(chunks[0], 0), chunks[1][q], chunks[2][q]]
            beside = logits_tick(q, now, head, sib, order, sums)
            early, *sums = ring_tick(chunks, "zxy", beside)
    now = [p[-1] for p in chunks]
    late, lb, lc, stats = logits_tick(SIDE - 1, now, head, sib, order, sums, metas, [early])
    la = [early, late]

    to_q = (sign * (z - quarter)) % SIDE
    pick = pick_rows(stats[1].reshape(SIDE, tok), to_q)
    square, count = SIDE**2, SIDE**3
    flat = jnp.concatenate(
        [
            jnp.broadcast_to(stats[0][None], (count, SIDE * tok)),
            jnp.broadcast_to(pick[:, None], (SIDE, square, tok)).reshape(count, tok),
            jnp.broadcast_to(loss_grad[None], (count, tok)),
        ],
        1,
    )
    flat, last = bar((flat, chunks[0]))
    xs = jnp.concatenate(last, 0), chunks[1], chunks[2]
    everyone = lax.all_to_all(flat, ("z", "y", "x"), 0, 0, tiled=True)
    losses, *dls = dlogits(everyone, la, lb, lc, metas, order)
    losses = losses.reshape(tok)

    n = dls[0].shape[0] // SIDE
    rest = jnp.concatenate([dls[0][2 * n :], dls[0][:n]], 0)
    sums = terms_tick(1, [dls[0][n : 2 * n], dls[1], dls[2]], head, sib, order)
    for q in (2, 3, 0):
        moved = [shift(s, axis, 1) for s, axis in zip(sums, "zxy")]
        if q == 2:
            others, *crossed = terms_tick(2, [rest, dls[1], dls[2]], head, sib, order)
            others = jnp.split(others, SIDE - 1, 0)
            moved, dls = bar((moved, dls))
            dlt = jnp.concatenate(dls, 0).T
        if q == 3:
            crossed = terms_cross(3, dls[1], dls[2], head, sib, order)
            final = terms_cross(0, dls[1], dls[2], head, sib, order)
            moved, dlt, final = bar((moved, dlt, final))
        if q == 0:
            crossed = final
            theirs = head_part(dlt[vocab:], *xs, order)
            moved, theirs = bar((moved, theirs))
        terms = [others[(q - 2) % SIDE], *crossed]
        sums = [(m.astype(F32) + t.astype(F32)).astype(BF16) for m, t in zip(moved, terms)]
    head_grad = head_part(dlt[:vocab], *xs, order, swap_cores(theirs))
    sums, head_grad = scatter_direct(sums, "yzx", (1, 0, 1), head_grad)
    sums, _ = scatter_direct(sums, "xyz", (1, 1, 0))
    hidden_grad = jnp.concatenate(sums, 0)
    return losses, hidden_grad, head_grad


def solution(mesh):
    grid = Mesh(mesh.devices.reshape(SIDE, CORES, SIDE, SIDE), AXES)
    dp, owners = ("z", "c"), ("y", "x")
    in_specs = (P(dp, owners), P(owners + dp, None), P(), P(), P(dp))
    out_specs = (P(dp), P(dp, owners), P(owners + dp, None))
    return jax.shard_map(
        on_device, mesh=grid, in_specs=in_specs, out_specs=out_specs, check_vma=False
    )
```
